128 devices in a mesh: row: 8 (over x, y_lo), col: 16 (over z, y_hi, core).
Axes of the slice: x: 4, y: 4 (y_hi: 2, y_lo: 2; y = y_hi * 2 + y_lo), z: 4, core: 2. Of those that a mesh axis runs over, the one named last changes fastest.
Arguments:
- input_a: bfloat16 [512, 12288], P('row', 'col'), may hold values from -6 to 6
- input_b: bfloat16 [512, 12288], P('row', 'col'), may hold values from -6 to 6
- cotangent: bfloat16 [512, 12288], P('row', 'col'), may hold values from -1.5 to 1.5
- weight_in: bfloat16 [12288, 24576], P('col', 'row'), may hold values from -0.0546875 to 0.0546875
- bias_in: float32 [24576], P('row'), may hold values from -3 to 3
- weight_out: bfloat16 [24576, 12288], P('row', 'col'), may hold values from -0.0390625 to 0.0390625
- bias_out: float32 [12288], P('col'), may hold values from -3 to 3
Outputs:
- output_a: bfloat16 [512, 12288], P('row', 'col')
- grad_input: bfloat16 [512, 12288], P('row', 'col')
- grad_weight_in: bfloat16 [12288, 24576], P('col', 'row')
- grad_bias_in: float32 [24576], P('row')
- grad_weight_out: bfloat16 [24576, 12288], P('row', 'col')
- grad_bias_out: float32 [12288], P('col')
The draws below stay inside these ranges and needn't reach their ends.
All inputs are finite; a program needn't handle non-finite values.
Results may differ from the reference program's by a relative error of at most 0.007.
Values may be sent and summed in bfloat16 or wider, within the bound.
No kernel may reach another device: no remote copies, remote signals or barrier semaphores. Data moves between devices by JAX's collectives and lax.ppermute only.
A program may use at most 128 MiB of HBM per device.

```python
import jax
import jax.numpy as jnp
from jax import lax

D = 12288
FF = 24576
TOKENS = 512


def block_levels(stream_key, extent, cuts, least, largest):
    def one(axis_at, blocks):
        draws = jax.random.uniform(jax.random.fold_in(jax.random.fold_in(stream_key, 6), axis_at), (blocks,), jnp.float32, least / len(cuts), largest / len(cuts))
        return jnp.repeat(jnp.exp(draws), extent[axis_at] // blocks).reshape((-1,) + (1,) * (len(extent) - axis_at - 1))

    gain = one(*cuts[0])
    for cut in cuts[1:]:
        gain = gain * one(*cut)
    return gain


def centred(key, dims, width, reach, cuts=(), kind=jnp.bfloat16):
    array = width * jax.random.normal(key, dims, jnp.float32)
    if cuts:
        array = array * block_levels(key, dims, cuts, -0.22, 0.18)
    return jnp.clip(array, -reach, reach).astype(kind)


def setup_inputs(seed: int = 0) -> dict:
    seeds = jax.random.split(jax.random.key(seed), 8)
    return {
        "input_a": centred(seeds[0], (TOKENS, D), 1.0, 6.0, ((0, 8), (1, 16))),
        "input_b": centred(seeds[1], (TOKENS, D), 1.0, 6.0, ((0, 8), (1, 16))),
        "cotangent": centred(seeds[2], (TOKENS, D), 0.25, 1.5, ((0, 8), (1, 16))),
        "weight_in": centred(seeds[3], (D, FF), D ** -0.5, 0.0546875, ((0, 16), (1, 8))),
        "bias_in": centred(seeds[4], (FF,), 0.5, 3.0, ((0, 8),), jnp.float32),
        "weight_out": centred(seeds[5], (FF, D), FF ** -0.5, 0.0390625, ((0, 8), (1, 16))),
        "bias_out": centred(seeds[6], (D,), 0.5, 3.0, ((0, 16),), jnp.float32),
    }


coeff = 0.7978845608


def gelu_tanh(values):
    return 0.5 * values * (1.0 + jnp.tanh(coeff * (values + 0.044715 * values * values * values)))


def gelu_slope(values):
    tangent = jnp.tanh(coeff * (values + 0.044715 * values * values * values))
    return 0.5 * (1.0 + tangent) + 0.5 * values * (1.0 - tangent * tangent) * coeff * (1.0 + 3.0 * 0.044715 * values * values)


def reference(input_a, input_b, cotangent, weight_in, bias_in, weight_out, bias_out):
    outer = (((0,), (0,)), ((), ()))
    inner = (((1,), (1,)), ((), ()))
    pre_a = jnp.dot(input_a, weight_in, preferred_element_type=jnp.float32) + bias_in
    hidden_a = gelu_tanh(pre_a).astype(jnp.bfloat16)
    output_a = (jnp.dot(hidden_a, weight_out, preferred_element_type=jnp.float32) + bias_out).astype(jnp.bfloat16)
    pre_b = jnp.dot(input_b, weight_in, preferred_element_type=jnp.float32) + bias_in
    hidden_b = gelu_tanh(pre_b).astype(jnp.bfloat16)
    grad_weight_out = lax.dot_general(hidden_b, cotangent, outer, preferred_element_type=jnp.float32).astype(jnp.bfloat16)
    grad_bias_out = jnp.sum(cotangent.astype(jnp.float32), axis=0)
    back_hidden = lax.dot_general(cotangent, weight_out, inner, preferred_element_type=jnp.float32)
    back_pre = (back_hidden * gelu_slope(pre_b)).astype(jnp.bfloat16)
    grad_bias_in = jnp.sum(back_pre.astype(jnp.float32), axis=0)
    grad_weight_in = lax.dot_general(input_b, back_pre, outer, preferred_element_type=jnp.float32).astype(jnp.bfloat16)
    grad_input = lax.dot_general(back_pre, weight_in, inner, preferred_element_type=jnp.float32).astype(jnp.bfloat16)
    return (output_a, grad_input, grad_weight_in, grad_bias_in, grad_weight_out, grad_bias_out)
```

```python
import jax
import jax.numpy as jnp
from jax import lax
from jax.sharding import Mesh, PartitionSpec as P

coeff = 0.7978845608
outer = (((0,), (0,)), ((), ()))
inner = (((1,), (1,)), ((), ()))
ROW = ("x", "yl")
CHIPS = ("z", "yh")
COL = ("z", "yh", "core")
f32 = jnp.float32
bf16 = jnp.bfloat16


def gelu_tanh(values):
    return 0.5 * values * (1.0 + jnp.tanh(coeff * (values + 0.044715 * values * values * values)))


def gelu_slope(values):
    tangent = jnp.tanh(coeff * (values + 0.044715 * values * values * values))
    return 0.5 * (1.0 + tangent) + 0.5 * values * (1.0 - tangent * tangent) * coeff * (
        1.0 + 3.0 * 0.044715 * values * values
    )


def swap(values):
    return lax.ppermute(values, "core", [(0, 1), (1, 0)])


def spread(values, axes):
    members = lax.axis_size(axes)
    return lax.all_to_all(jnp.broadcast_to(values, (members,) + values.shape), axes, 0, 0)


def collect(parts, axes):
    return jnp.sum(lax.all_to_all(parts, axes, 0, 0).astype(f32), axis=0)


def tokens_of(values):
    count, width = values.shape
    half = count // 2
    core = lax.axis_index("core")
    mine = lax.dynamic_slice(values, (core * half, 0), (half, width))
    other = lax.dynamic_slice(values, ((1 - core) * half, 0), (half, width))
    rows = spread(jnp.concatenate([mine, other], 0), ROW)
    return rows[:, :half].reshape(-1, width), rows[:, half:].reshape(-1, width)


def sum_features(pair, weight, dims):
    mine, other = pair
    sent = swap(lax.dot_general(other, weight, dims, preferred_element_type=f32).astype(bf16))
    kept = lax.dot_general(mine, weight, dims, preferred_element_type=f32)
    both = (kept + sent.astype(f32)).astype(bf16)
    chips = lax.axis_size(CHIPS)
    return collect(both.reshape(chips, both.shape[0] // chips, both.shape[1]), CHIPS)


def all_tokens(values):
    mine = spread(values, CHIPS).reshape(-1, values.shape[1])
    return mine, swap(mine)


def sum_hidden(mine, other):
    rows = lax.axis_size(ROW)
    width = mine.shape[1]
    half = mine.shape[0] // rows
    parts = jnp.concatenate([mine.reshape(rows, half, width), other.reshape(rows, half, width)], 1)
    total = collect(parts, ROW)
    core = lax.axis_index("core")
    return lax.dynamic_slice(jnp.concatenate([total, total[:half]], 0), (core * half, 0), (2 * half, width))


plain = (((1,), (0,)), ((), ()))


def per_device(input_a, input_b, cotangent, weight_in, bias_in, weight_out, bias_out):
    rows_b = tokens_of(input_b)
    rows_cot = tokens_of(cotangent)
    rows_a = tokens_of(input_a)
    pre_b = sum_features(rows_b, weight_in, plain) + bias_in
    back_hidden = sum_features(rows_cot, weight_out, inner)
    pre_a = sum_features(rows_a, weight_in, plain) + bias_in
    back_pre = (back_hidden * gelu_slope(pre_b)).astype(bf16)
    hidden_b = gelu_tanh(pre_b).astype(bf16)
    hidden_a = gelu_tanh(pre_a).astype(bf16)

    full_back = all_tokens(back_pre)
    full_a = all_tokens(hidden_a)
    full_b = all_tokens(hidden_b)

    def both(pair):
        return jnp.concatenate(pair, 0)

    grad_input = sum_hidden(
        *[lax.dot_general(v, weight_in, inner, preferred_element_type=f32).astype(bf16) for v in full_back]
    ).astype(bf16)
    output_a = (
        sum_hidden(
            *[lax.dot_general(v, weight_out, plain, preferred_element_type=f32).astype(bf16) for v in full_a]
        )
        + bias_out
    ).astype(bf16)
    all_back = both(full_back)
    all_cot = both(rows_cot)
    grad_weight_in = lax.dot_general(
        both(rows_b), all_back, outer, preferred_element_type=f32
    ).astype(bf16)
    grad_bias_in = jnp.sum(all_back.astype(f32), axis=0)
    grad_weight_out = lax.dot_general(
        both(full_b), all_cot, outer, preferred_element_type=f32
    ).astype(bf16)
    grad_bias_out = jnp.sum(all_cot.astype(f32), axis=0)
    return (output_a, grad_input, grad_weight_in, grad_bias_in, grad_weight_out, grad_bias_out)


def solution(mesh):
    fine = Mesh(mesh.devices.reshape(4, 2, 4, 2, 2), ("x", "yl", "z", "yh", "core"))
    return jax.shard_map(
        per_device,
        mesh=fine,
        in_specs=(
            P(ROW, COL),
            P(ROW, COL),
            P(ROW, COL),
            P(COL, ROW),
            P(ROW),
            P(ROW, COL),
            P(COL),
        ),
        out_specs=(
            P(ROW, COL),
            P(ROW, COL),
            P(COL, ROW),
            P(ROW),
            P(ROW, COL),
            P(COL),
        ),
        check_vma=False,
    )
```

```python
import functools

import jax
import jax.numpy as jnp
from jax import lax
from jax.experimental import pallas as pl
from jax.experimental.pallas import tpu as pltpu
from jax.sharding import Mesh, PartitionSpec as P

coeff = 0.7978845608
plain = (((1,), (0,)), ((), ()))
outer = (((0,), (0,)), ((), ()))
inner = (((1,), (1,)), ((), ()))
ROW = ("x", "yl")
CHIPS = ("z", "yh")
COL = ("z", "yh", "core")
f32 = jnp.float32
bf16 = jnp.bfloat16
VMEM_LIMIT = 40 << 20
ALL_VMEM = 61 << 20
MICRO = 3_000
TILE = 512


def gelu_tanh(values):
    return 0.5 * values * (1.0 + jnp.tanh(coeff * (values + 0.044715 * values * values * values)))


def gelu_slope(values):
    tangent = jnp.tanh(coeff * (values + 0.044715 * values * values * values))
    return 0.5 * (1.0 + tangent) + 0.5 * values * (1.0 - tangent * tangent) * coeff * (
        1.0 + 3.0 * 0.044715 * values * values
    )


def swap(values, axis="core", name="core_swap"):
    with jax.named_scope(name):
        return lax.ppermute(values, axis, [(0, 1), (1, 0)])


def whole(array):
    return pl.BlockSpec(array.shape, lambda j, core: (0,) * len(array.shape))


def tiled(array, axis, tile, at=lambda j, core: j):
    shape = array.shape[:axis] + (tile,) + array.shape[axis + 1 :]
    return pl.BlockSpec(shape, lambda j, core: tuple(at(j, core[0]) if i == axis else 0 for i in range(len(shape))))


def last(array, tile, at=lambda j, core: j):
    return tiled(array, len(array.shape) - 1, tile, at)


def like(shape, dtype=bf16):
    return jax.ShapeDtypeStruct(shape, dtype)


def call(body, steps, operands, in_specs, shapes, out_specs, waits=(), scratch=(), micros=1, limit=VMEM_LIMIT):
    used = len(operands)
    name = body.__qualname__.split(".")[0]

    def kernel(core, *refs):
        body(*refs[:used], *refs[used + len(waits) :])

    return pl.pallas_call(
        kernel,
        name=name,
        grid_spec=pltpu.PrefetchScalarGridSpec(
            num_scalar_prefetch=1,
            grid=(steps,),
            in_specs=[*in_specs, *[pl.BlockSpec(memory_space=pl.ANY)] * len(waits)],
            out_specs=out_specs,
            scratch_shapes=scratch,
        ),
        out_shape=shapes,
        compiler_params=pltpu.CompilerParams(vmem_limit_bytes=limit),
        cost_estimate=pl.CostEstimate(flops=0, bytes_accessed=micros * MICRO, transcendentals=0),
    )(lax.axis_index("core").astype(jnp.int32)[None], *operands, *waits)


def spread_kernel(x, out):
    sub = out.shape[2]
    for a in range(2):
        piece = x[pl.ds(pl.multiple_of((lax.axis_index("yh") ^ a) * sub, sub), sub), :]
        for i in range(out.shape[0]):
            out[i, a] = piece


def tokens_of(values, name, waits=()):
    count, width = values.shape
    shape = like((lax.axis_size(ROW), 2, count // 2, width))
    (copies,) = call(spread_kernel, 1, [values], [whole(values)], [shape], [whole(shape)], waits)
    with jax.named_scope(name):
        return lax.all_to_all(copies, ROW, 0, 0), copies


def tokens_of_chip(values, waits=()):
    def body(x, out):
        sub = out.shape[1]
        for a in range(2):
            out[a] = x[pl.ds(pl.multiple_of((lax.axis_index("yh") ^ a) * sub, sub), sub), :]

    count, width = values.shape
    ordered = simple(body, [values], [like((2, count // 2, width))], waits)[0]
    found = lax.all_gather(ordered, (*ROW, "core"), axis=0, tiled=False)
    return found.reshape(-1, 2, *ordered.shape)


def settle_kernel(parts, bias, out):
    sub = parts.shape[1] // 2
    total = jnp.sum(parts[...].astype(f32), axis=0) + bias[...]
    for a in range(2):
        at = pl.ds(pl.multiple_of((lax.axis_index("yh") ^ a) * sub, sub), sub)
        out[at, :] = total[a * sub : (a + 1) * sub].astype(bf16)


def sum_hidden(parts, bias, name, waits=()):
    rows, subs, sub, width = parts.shape
    with jax.named_scope(name):
        got = lax.all_to_all(parts, ROW, 0, 0).reshape(rows, subs * sub, width)
    shape = like((subs * sub, width))
    (out,) = call(settle_kernel, 1, [got, bias], [whole(got), whole(bias)], [shape], [whole(shape)], waits)
    return out


def rows_of(ref):
    rows, _, sub, width = ref.shape
    return jnp.concatenate([ref[:, a].reshape(rows * sub, width) for a in range(2)], 0)


IN_HBM = pl.BlockSpec(memory_space=pltpu.HBM)


def part_of(weight, axis, start, size):
    at = pl.ds(pl.multiple_of(start, size), size)
    return weight.at[:, at] if axis else weight.at[at, :]


def exchanged(weight, axis, waits, tile=TILE):
    def body(part, out):
        out[...] = part[...]

    half = weight.shape[axis] // 2
    steps = half // tile
    shape = like(weight.shape[:axis] + (half,) + weight.shape[axis + 1 :])
    spec = tiled(weight, axis, tile, lambda j, core: (1 - core) * steps + j)
    return swap(call(body, steps, [weight], [spec], [shape], [tiled(shape, axis, tile)], waits)[0])


def fetched(pairs, axis, tile, steps):
    shapes = [a.shape[:axis] + (tile,) + a.shape[axis + 1 :] for a in pairs]
    scratch = [pltpu.VMEM((steps,) + shape, bf16) for shape in shapes]
    scratch += [pltpu.SemaphoreType.DMA((steps,)) for _ in pairs]

    def get(refs, firsts, buffers, sems):
        step = pl.program_id(0)

        def copy(k, j):
            return pltpu.make_async_copy(
                part_of(refs[k], axis, (firsts[k] + j) * tile, tile), buffers[k].at[j], sems[k].at[j]
            )

        @pl.when(step == 0)
        def _():
            for j in range(steps):
                for k in range(len(refs)):
                    copy(k, j).start()

        for k in range(len(refs)):
            copy(k, step).wait()
        return [buffer[step] for buffer in buffers]

    return scratch, get


def up(x, w, w_far, dims, kind, waits=(), tile=TILE):
    axis = 1 if dims == plain else 0
    half = w_far.shape[axis]
    steps = half // tile
    chips = lax.axis_size("z")

    scratch, get = fetched([w, w_far], axis, tile, steps)

    def body(x, x_far, *refs):
        *outs, own, own_far, sem, sem_far = refs[2:]
        w, w_far = get(refs[:2], [lax.axis_index("core") * steps, 0], [own, own_far], [sem, sem_far])
        term = lax.dot_general(rows_of(x), w, dims, preferred_element_type=f32)
        term += lax.dot_general(rows_of(x_far), w_far, dims, preferred_element_type=f32)
        count = term.shape[0] // 2
        for a in range(2):
            part = term[a * count : (a + 1) * count].astype(bf16)
            if kind == "pair":
                outs[a][...] = part
            else:
                outs[0][:, a] = part.reshape(chips, count // chips, tile)

    if len(x) == 2:
        specs = [whole(x[0]), whole(x[1])]
    else:
        x = (x[0], x[0])
        rows, _, subs, sub, width = x[0].shape
        specs = [pl.BlockSpec((rows, None, subs, sub, width), lambda j, core, k=k: (0, core[0] ^ k, 0, 0, 0)) for k in range(2)]
    rows, subs, sub, width = x[0].shape[-4:] if len(x[0].shape) == 4 else (x[0].shape[0], *x[0].shape[2:])
    if kind == "pair":
        shapes = [like((rows * sub, half))] * 2
    else:
        shapes = [like((chips, 2, rows * sub // chips, half))]
    specs += [IN_HBM, IN_HBM]
    return call(body, steps, [*x, w, w_far], specs, shapes, [last(s, tile) for s in shapes], waits, scratch, 5, ALL_VMEM)


def all_rows(refs, kind):
    if kind == "quarters":
        return jnp.concatenate([ref[...] for ref in refs], 0)
    (ref,) = refs
    chips, _, block, width = ref.shape
    order = [a if kind == "relative" else lax.axis_index("yh") ^ a for a in range(2)]
    return jnp.concatenate([ref[:, pl.ds(at, 1)].reshape(chips * block, width) for at in order], 0)


def down(full, w, dims, x, waits=(), tile=TILE):
    near, far, kind = full
    axis = 0 if dims == plain else 1
    steps = near[0].shape[-1] // tile
    count = len(near)

    scratch, get = fetched([w, w], axis, tile, steps)

    def body(*refs):
        *parts, w, out, total, own, own_far, sem, sem_far = refs
        step = pl.program_id(0)
        core = lax.axis_index("core")
        w_near, w_far = get([w, w], [core * steps, (1 - core) * steps], [own, own_far], [sem, sem_far])
        term = lax.dot_general(all_rows(parts[:count], kind), w_near, dims, preferred_element_type=f32)
        term += lax.dot_general(all_rows(parts[count:], kind), w_far, dims, preferred_element_type=f32)

        @pl.when(step == 0)
        def _():
            total[...] = term

        @pl.when(step > 0)
        def _():
            total[...] += term

        @pl.when(step == steps - 1)
        def _():
            rows, _, sub, width = out.shape
            for a in range(2):
                out[:, a] = total[a * rows * sub : (a + 1) * rows * sub].astype(bf16).reshape(rows, sub, width)

    shape = like(x.shape)
    specs = [last(h, tile) for h in (*near, *far)]
    specs += [IN_HBM]
    scratch = [pltpu.VMEM((x.size // x.shape[-1], x.shape[-1]), f32), *scratch]
    return call(body, steps, [*near, *far, w], specs, [shape], [whole(shape)], waits, scratch, 6, ALL_VMEM)[0]


def grad(x, full, along, sums=False, waits=(), tile=TILE):
    near, far, kind = full
    half, width = near[0].shape[-1], x.shape[-1]
    steps = half // tile
    count = len(near)

    def body(x, *refs):
        parts, outs = refs[: 2 * count], refs[2 * count :]

        def one(refs):
            values = all_rows(refs, kind)
            pair = (values, rows_of(x)) if along == 0 else (rows_of(x), values)
            outs[0][...] = lax.dot_general(*pair, outer, preferred_element_type=f32).astype(bf16)
            if sums:
                outs[1][...] = jnp.sum(values.astype(f32), axis=0, keepdims=True)

        @pl.when(pl.program_id(0) < steps)
        def _():
            one(parts[:count])

        @pl.when(pl.program_id(0) >= steps)
        def _():
            one(parts[count:])

    def place(j, core):
        return jnp.where(j < steps, core * steps + j, (1 - core) * steps + j - steps)

    shape = like((width, 2 * half) if along else (2 * half, width))
    shapes = [shape] + ([like((1, 2 * half), f32)] if sums else [])
    out_specs = [tiled(shape, along, tile, place)] + ([last(shapes[1], tile, place)] if sums else [])
    specs = [whole(x), *[last(h, tile, lambda j, core: jnp.minimum(j, steps - 1)) for h in near]]
    specs += [last(h, tile, lambda j, core: jnp.maximum(j - steps, 0)) for h in far]
    return call(body, 2 * steps, [x, *near, *far], specs, shapes, out_specs, waits, (), 6)


def simple(body, operands, shapes, waits=()):
    return call(body, 1, operands, [whole(o) for o in operands], shapes, [whole(s) for s in shapes], waits)


def add_far(kept, got, waits=()):
    def body(kept, got, out):
        out[...] = (kept[...].astype(f32) + got[...].astype(f32)).astype(bf16)

    return simple(body, [kept, got], [like(kept.shape)], waits)[0]


def halves_of(got, waits=()):
    def body(got, kept, sent):
        kept[...] = jnp.sum(got[:, 0].astype(f32), axis=0)
        sent[...] = jnp.sum(got[:, 1].astype(f32), axis=0).astype(bf16)

    return simple(body, [got], [like(got.shape[2:], f32), like(got.shape[2:])], waits)


def finish_b(near, far, bias, waits=()):
    def body(near, far, bias, pre, out):
        values = near[...] + far[...].astype(f32) + bias[...]
        pre[...] = values
        out[...] = gelu_tanh(values).astype(bf16)

    return simple(body, [near, far, bias], [like(near.shape, f32), like(near.shape)], waits)


def finish_a(got, bias, copies, waits=()):
    def body(got, bias, out):
        values = gelu_tanh(jnp.sum(got[...].astype(f32), axis=0) + bias[...]).astype(bf16)
        for i in range(copies):
            out[i] = values

    return simple(body, [got, bias], [like((copies,) + got.shape[1:])], waits)[0]


def finish_back(got, pre, copies, waits=()):
    def body(got, pre, out):
        back = jnp.sum(got[...].astype(f32), axis=0)
        values = (back * gelu_slope(pre[...])).astype(bf16)
        for i in range(copies):
            out[i] = values

    return simple(body, [got, pre], [like((copies,) + pre.shape)], waits)[0]


def paired(near, far, copies, waits=()):
    def body(near, far, out):
        for i in range(copies):
            out[i, 0] = near[...]
            out[i, 1] = far[...]

    return simple(body, [near, far], [like((copies, 2) + near.shape)], waits)[0]


def relay(values, waits):
    def body(x, out):
        out[...] = x[...]

    return simple(body, [values], [like(values.shape)], waits)[0]


def along_z(values, name):
    with jax.named_scope(name):
        return lax.all_to_all(values, "z", 0, 0)


def gather_near(copies, name, waits=()):
    near = along_z(copies, name + "_z").reshape(-1, copies.shape[-1])
    far = swap(near, "yh", name + "_y")
    passed = relay(far, waits) if waits else far
    return [near, far], [swap(near), swap(passed)], "quarters"


def gather_far(values, name, waits=(), waits_core=()):
    mine = along_z(paired(values, swap(values, "yh", name + "_y"), lax.axis_size("z"), waits), name + "_z")
    passed = relay(mine, waits_core) if waits_core else mine
    return [mine], [swap(passed)], "relative"


def per_device(input_a, input_b, cotangent, weight_in, bias_in, weight_out, bias_out):
    hidden = weight_in.shape[1]
    chips = lax.axis_size("z")
    bias_out = bias_out[None]
    bias_half = lax.dynamic_slice_in_dim(bias_in, lax.axis_index("core") * (hidden // 2), hidden // 2)[None]

    x_a, _ = tokens_of(input_a, "row_a")
    x_b, _ = tokens_of(input_b, "row_b")
    x_cot, _ = tokens_of(cotangent, "row_cot")
    far_in = exchanged(weight_in, 1, [x_a])

    kept_a, sent_a = up([x_a, swap(x_a)], weight_in, far_in, plain, "pair")
    far_out = exchanged(weight_out, 0, [kept_a])
    (term_b,) = up([x_b, swap(relay(x_b, [kept_a]))], weight_in, far_in, plain, "relative")
    kept_cot, sent_cot = up([x_cot, swap(relay(x_cot, [term_b]))], weight_out, far_out, inner, "pair")

    near_b, sent_b = halves_of(along_z(term_b, "sum_b_z"), [kept_cot])
    both_a = add_far(kept_a, swap(sent_a, "yh", "sum_a_y"), [near_b])
    got_a = along_z(both_a.reshape(chips, -1, hidden // 2), "sum_a_z")
    both_cot = add_far(kept_cot, swap(sent_cot, "yh", "sum_cot_y"))
    pre_b, hidden_b = finish_b(near_b, swap(sent_b, "yh", "sum_b_y"), bias_half)
    copies_a = finish_a(got_a, bias_half, chips, [pre_b])
    full_a = gather_near(copies_a, "all_a")
    got_cot = along_z(both_cot.reshape(chips, -1, hidden // 2), "sum_cot_z")
    copies_back = finish_back(got_cot, pre_b, chips, [copies_a])

    parts_a = down(full_a, weight_out, plain, x_b, [copies_back])
    full_back = gather_near(copies_back, "all_back", [parts_a])
    full_b = gather_far(hidden_b, "all_b", [full_a[0][1], full_back[0][0]], [parts_a, full_back[0][1]])
    (grad_weight_out,) = grad(x_cot, full_b, 0, False, [parts_a])
    parts_back = down(full_back, weight_in, inner, x_b, [grad_weight_out])
    grad_weight_in, sums = grad(x_b, full_back, 1, True, [parts_back])
    output_a = sum_hidden(parts_a, bias_out, "row_out")
    grad_input = sum_hidden(parts_back, jnp.zeros_like(bias_out), "row_in")
    grad_bias_out = jnp.sum(x_cot.reshape(-1, x_cot.shape[-1]).astype(f32), axis=0)
    return (output_a, grad_input, grad_weight_in, sums[0], grad_weight_out, grad_bias_out)


def solution(mesh):
    fine = Mesh(mesh.devices.reshape(4, 2, 4, 2, 2), ("x", "yl", "z", "yh", "core"))
    return jax.shard_map(
        per_device,
        mesh=fine,
        in_specs=(
            P(ROW, COL),
            P(ROW, COL),
            P(ROW, COL),
            P(COL, ROW),
            P(ROW),
            P(ROW, COL),
            P(COL),
        ),
        out_specs=(
            P(ROW, COL),
            P(ROW, COL),
            P(COL, ROW),
            P(ROW),
            P(ROW, COL),
            P(COL),
        ),
        check_vma=False,
    )
```

```python
import functools

import jax
import jax.numpy as jnp
from jax import lax
from jax.experimental import pallas as pl
from jax.experimental.pallas import tpu as pltpu
from jax.sharding import Mesh, PartitionSpec as P

coeff = 0.7978845608
plain = (((1,), (0,)), ((), ()))
outer = (((0,), (0,)), ((), ()))
inner = (((1,), (1,)), ((), ()))
ROW = ("x", "yl")
CHIPS = ("z", "yh")
COL = ("z", "yh", "core")
f32 = jnp.float32
bf16 = jnp.bfloat16
VMEM_LIMIT = 40 << 20
ALL_VMEM = 61 << 20
MICRO = 3_000
TILE = 768


def gelu_tanh(values):
    return 0.5 * values * (1.0 + jnp.tanh(coeff * (values + 0.044715 * values * values * values)))


def gelu_slope(values):
    tangent = jnp.tanh(coeff * (values + 0.044715 * values * values * values))
    return 0.5 * (1.0 + tangent) + 0.5 * values * (1.0 - tangent * tangent) * coeff * (
        1.0 + 3.0 * 0.044715 * values * values
    )


def swap(values, axis="core", name="core_swap"):
    with jax.named_scope(name):
        return lax.ppermute(values, axis, [(0, 1), (1, 0)])


def whole(array):
    return pl.BlockSpec(array.shape, lambda j, core: (0,) * len(array.shape))


def tiled(array, axis, tile, at=lambda j, core: j):
    shape = array.shape[:axis] + (tile,) + array.shape[axis + 1 :]
    return pl.BlockSpec(shape, lambda j, core: tuple(at(j, core[0]) if i == axis else 0 for i in range(len(shape))))


def last(array, tile, at=lambda j, core: j):
    return tiled(array, len(array.shape) - 1, tile, at)


def like(shape, dtype=bf16):
    return jax.ShapeDtypeStruct(shape, dtype)


def call(body, steps, operands, in_specs, shapes, out_specs, waits=(), scratch=(), micros=1, limit=VMEM_LIMIT):
    used = len(operands)
    name = body.__qualname__.split(".")[0]

    def kernel(core, *refs):
        body(*refs[:used], *refs[used + len(waits) :])

    return pl.pallas_call(
        kernel,
        name=name,
        grid_spec=pltpu.PrefetchScalarGridSpec(
            num_scalar_prefetch=1,
            grid=(steps,),
            in_specs=[*in_specs, *[pl.BlockSpec(memory_space=pl.ANY)] * len(waits)],
            out_specs=out_specs,
            scratch_shapes=scratch,
        ),
        out_shape=shapes,
        compiler_params=pltpu.CompilerParams(vmem_limit_bytes=limit),
        cost_estimate=pl.CostEstimate(flops=0, bytes_accessed=micros * MICRO, transcendentals=0),
    )(lax.axis_index("core").astype(jnp.int32)[None], *operands, *waits)


def spread_kernel(x, out):
    sub = out.shape[2]
    for a in range(2):
        piece = x[pl.ds(pl.multiple_of((lax.axis_index("yh") ^ a) * sub, sub), sub), :]
        for i in range(out.shape[0]):
            out[i, a] = piece


def tokens_of(values, name, waits=()):
    count, width = values.shape
    shape = like((lax.axis_size(ROW), 2, count // 2, width))
    (copies,) = call(spread_kernel, 1, [values], [whole(values)], [shape], [whole(shape)], waits)
    with jax.named_scope(name):
        return lax.all_to_all(copies, ROW, 0, 0), copies


def tokens_of_chip(values, waits=()):
    def body(x, out):
        sub = out.shape[1]
        for a in range(2):
            out[a] = x[pl.ds(pl.multiple_of((lax.axis_index("yh") ^ a) * sub, sub), sub), :]

    count, width = values.shape
    ordered = simple(body, [values], [like((2, count // 2, width))], waits)[0]
    found = lax.all_gather(ordered, (*ROW, "core"), axis=0, tiled=False)
    return found.reshape(-1, 2, *ordered.shape)


def settle_kernel(parts, bias, out):
    sub = parts.shape[1] // 2
    total = jnp.sum(parts[...].astype(f32), axis=0) + bias[...]
    for a in range(2):
        at = pl.ds(pl.multiple_of((lax.axis_index("yh") ^ a) * sub, sub), sub)
        out[at, :] = total[a * sub : (a + 1) * sub].astype(bf16)


def sum_hidden(parts, bias, name, waits=()):
    rows, subs, sub, width = parts.shape
    with jax.named_scope(name):
        got = lax.all_to_all(parts, ROW, 0, 0).reshape(rows, subs * sub, width)
    shape = like((subs * sub, width))
    (out,) = call(settle_kernel, 1, [got, bias], [whole(got), whole(bias)], [shape], [whole(shape)], waits)
    return out


def rows_of(ref):
    rows, _, sub, width = ref.shape
    return jnp.concatenate([ref[:, a].reshape(rows * sub, width) for a in range(2)], 0)


IN_HBM = pl.BlockSpec(memory_space=pltpu.HBM)


def part_of(weight, axis, start, size):
    at = pl.ds(pl.multiple_of(start, size), size)
    return weight.at[:, at] if axis else weight.at[at, :]


def exchanged(weight, axis, waits, tile=TILE):
    def body(part, out):
        out[...] = part[...]

    half = weight.shape[axis] // 2
    steps = half // tile
    shape = like(weight.shape[:axis] + (half,) + weight.shape[axis + 1 :])
    spec = tiled(weight, axis, tile, lambda j, core: (1 - core) * steps + j)
    return swap(call(body, steps, [weight], [spec], [shape], [tiled(shape, axis, tile)], waits)[0])


def fetched(pairs, axis, tile, steps):
    shapes = [a.shape[:axis] + (tile,) + a.shape[axis + 1 :] for a in pairs]
    scratch = [pltpu.VMEM((steps,) + shape, bf16) for shape in shapes]
    scratch += [pltpu.SemaphoreType.DMA((steps,)) for _ in pairs]

    def get(refs, firsts, buffers, sems):
        step = pl.program_id(0)

        def copy(k, j):
            return pltpu.make_async_copy(
                part_of(refs[k], axis, (firsts[k] + j) * tile, tile), buffers[k].at[j], sems[k].at[j]
            )

        @pl.when(step == 0)
        def _():
            for j in range(steps):
                for k in range(len(refs)):
                    copy(k, j).start()

        for k in range(len(refs)):
            copy(k, step).wait()
        return [buffer[step] for buffer in buffers]

    return scratch, get


def up(x, w, w_far, dims, kind, waits=(), tile=TILE):
    axis = 1 if dims == plain else 0
    half = w_far.shape[axis]
    steps = half // tile
    chips = lax.axis_size("z")

    scratch, get = fetched([w, w_far], axis, tile, steps)

    def body(x, x_far, *refs):
        *outs, own, own_far, sem, sem_far = refs[2:]
        w, w_far = get(refs[:2], [lax.axis_index("core") * steps, 0], [own, own_far], [sem, sem_far])
        term = lax.dot_general(rows_of(x), w, dims, preferred_element_type=f32)
        term += lax.dot_general(rows_of(x_far), w_far, dims, preferred_element_type=f32)
        count = term.shape[0] // 2
        for a in range(2):
            part = term[a * count : (a + 1) * count].astype(bf16)
            if kind == "pair":
                outs[a][...] = part
            else:
                outs[0][:, a] = part.reshape(chips, count // chips, tile)

    if len(x) == 2:
        specs = [whole(x[0]), whole(x[1])]
    else:
        x = (x[0], x[0])
        rows, _, subs, sub, width = x[0].shape
        specs = [pl.BlockSpec((rows, None, subs, sub, width), lambda j, core, k=k: (0, core[0] ^ k, 0, 0, 0)) for k in range(2)]
    rows, subs, sub, width = x[0].shape[-4:] if len(x[0].shape) == 4 else (x[0].shape[0], *x[0].shape[2:])
    if kind == "pair":
        shapes = [like((rows * sub, half))] * 2
    else:
        shapes = [like((chips, 2, rows * sub // chips, half))]
    specs += [IN_HBM, IN_HBM]
    return call(body, steps, [*x, w, w_far], specs, shapes, [last(s, tile) for s in shapes], waits, scratch, 5, ALL_VMEM)


def all_rows(refs, kind):
    if kind == "quarters":
        return jnp.concatenate([ref[...] for ref in refs], 0)
    (ref,) = refs
    chips, _, block, width = ref.shape
    order = [a if kind == "relative" else lax.axis_index("yh") ^ a for a in range(2)]
    return jnp.concatenate([ref[:, pl.ds(at, 1)].reshape(chips * block, width) for at in order], 0)


def down(full, w, dims, x, waits=(), tile=TILE):
    near, far, kind = full
    axis = 0 if dims == plain else 1
    steps = near[0].shape[-1] // tile
    count = len(near)

    scratch, get = fetched([w, w], axis, tile, steps)

    def body(*refs):
        *parts, w, out, total, own, own_far, sem, sem_far = refs
        step = pl.program_id(0)
        core = lax.axis_index("core")
        w_near, w_far = get([w, w], [core * steps, (1 - core) * steps], [own, own_far], [sem, sem_far])
        term = lax.dot_general(all_rows(parts[:count], kind), w_near, dims, preferred_element_type=f32)
        term += lax.dot_general(all_rows(parts[count:], kind), w_far, dims, preferred_element_type=f32)

        @pl.when(step == 0)
        def _():
            total[...] = term

        @pl.when(step > 0)
        def _():
            total[...] += term

        @pl.when(step == steps - 1)
        def _():
            rows, _, sub, width = out.shape
            for a in range(2):
                out[:, a] = total[a * rows * sub : (a + 1) * rows * sub].astype(bf16).reshape(rows, sub, width)

    shape = like(x.shape)
    specs = [last(h, tile) for h in (*near, *far)]
    specs += [IN_HBM]
    scratch = [pltpu.VMEM((x.size // x.shape[-1], x.shape[-1]), f32), *scratch]
    return call(body, steps, [*near, *far, w], specs, [shape], [whole(shape)], waits, scratch, 6, ALL_VMEM)[0]


def grad(x, full, along, sums=False, waits=(), tile=TILE):
    near, far, kind = full
    half, width = near[0].shape[-1], x.shape[-1]
    steps = half // tile
    count = len(near)

    def body(x, *refs):
        parts, outs = refs[: 2 * count], refs[2 * count :]

        def one(refs):
            values = all_rows(refs, kind)
            pair = (values, rows_of(x)) if along == 0 else (rows_of(x), values)
            outs[0][...] = lax.dot_general(*pair, outer, preferred_element_type=f32).astype(bf16)
            if sums:
                outs[1][...] = jnp.sum(values.astype(f32), axis=0, keepdims=True)

        @pl.when(pl.program_id(0) < steps)
        def _():
            one(parts[:count])

        @pl.when(pl.program_id(0) >= steps)
        def _():
            one(parts[count:])

    def place(j, core):
        return jnp.where(j < steps, core * steps + j, (1 - core) * steps + j - steps)

    shape = like((width, 2 * half) if along else (2 * half, width))
    shapes = [shape] + ([like((1, 2 * half), f32)] if sums else [])
    out_specs = [tiled(shape, along, tile, place)] + ([last(shapes[1], tile, place)] if sums else [])
    specs = [whole(x), *[last(h, tile, lambda j, core: jnp.minimum(j, steps - 1)) for h in near]]
    specs += [last(h, tile, lambda j, core: jnp.maximum(j - steps, 0)) for h in far]
    return call(body, 2 * steps, [x, *near, *far], specs, shapes, out_specs, waits, (), 6)


def simple(body, operands, shapes, waits=()):
    return call(body, 1, operands, [whole(o) for o in operands], shapes, [whole(s) for s in shapes], waits)


def add_far(kept, got, waits=()):
    def body(kept, got, out):
        out[...] = (kept[...].astype(f32) + got[...].astype(f32)).astype(bf16)

    return simple(body, [kept, got], [like(kept.shape)], waits)[0]


def halves_of(got, waits=()):
    def body(got, kept, sent):
        kept[...] = jnp.sum(got[:, 0].astype(f32), axis=0)
        sent[...] = jnp.sum(got[:, 1].astype(f32), axis=0).astype(bf16)

    return simple(body, [got], [like(got.shape[2:], f32), like(got.shape[2:])], waits)


def finish_b(near, far, bias, waits=()):
    def body(near, far, bias, pre, out):
        values = near[...] + far[...].astype(f32) + bias[...]
        pre[...] = values
        out[...] = gelu_tanh(values).astype(bf16)

    return simple(body, [near, far, bias], [like(near.shape, f32), like(near.shape)], waits)


def finish_a(got, bias, copies, waits=()):
    def body(got, bias, out):
        values = gelu_tanh(jnp.sum(got[...].astype(f32), axis=0) + bias[...]).astype(bf16)
        for i in range(copies):
            out[i] = values

    return simple(body, [got, bias], [like((copies,) + got.shape[1:])], waits)[0]


def finish_back(got, pre, copies, waits=()):
    def body(got, pre, out):
        back = jnp.sum(got[...].astype(f32), axis=0)
        values = (back * gelu_slope(pre[...])).astype(bf16)
        for i in range(copies):
            out[i] = values

    return simple(body, [got, pre], [like((copies,) + pre.shape)], waits)[0]


def paired(near, far, copies, waits=()):
    def body(near, far, out):
        for i in range(copies):
            out[i, 0] = near[...]
            out[i, 1] = far[...]

    return simple(body, [near, far], [like((copies, 2) + near.shape)], waits)[0]


def copied(values, copies, waits):
    def body(x, out):
        for i in range(copies):
            out[i] = x[...]

    return simple(body, [values], [like((copies,) + values.shape)], waits)[0]


def relay(values, waits):
    def body(x, out):
        out[...] = x[...]

    return simple(body, [values], [like(values.shape)], waits)[0]


def along_z(values, name):
    with jax.named_scope(name):
        return lax.all_to_all(values, "z", 0, 0)


def gather_near(copies, name, waits=()):
    near = along_z(copies, name + "_z").reshape(-1, copies.shape[-1])
    far = swap(near, "yh", name + "_y")
    passed = relay(far, waits) if waits else far
    return [near, far], [swap(near), swap(passed)], "quarters"


def gather_far(values, name, waits=(), waits_core=()):
    mine = along_z(paired(values, swap(values, "yh", name + "_y"), lax.axis_size("z"), waits), name + "_z")
    passed = relay(mine, waits_core) if waits_core else mine
    return [mine], [swap(passed)], "relative"


def per_device(input_a, input_b, cotangent, weight_in, bias_in, weight_out, bias_out):
    hidden = weight_in.shape[1]
    chips = lax.axis_size("z")
    bias_out = bias_out[None]
    bias_half = lax.dynamic_slice_in_dim(bias_in, lax.axis_index("core") * (hidden // 2), hidden // 2)[None]

    x_a, _ = tokens_of(input_a, "row_a")
    x_b, _ = tokens_of(input_b, "row_b")
    x_cot, _ = tokens_of(cotangent, "row_cot")
    far_in = exchanged(weight_in, 1, [x_a])

    kept_a, sent_a = up([x_a, swap(x_a)], weight_in, far_in, plain, "pair")
    far_out = exchanged(weight_out, 0, [kept_a])
    (term_b,) = up([x_b, swap(relay(x_b, [kept_a]))], weight_in, far_in, plain, "relative")
    kept_cot, sent_cot = up([x_cot, swap(relay(x_cot, [term_b]))], weight_out, far_out, inner, "pair")

    near_b, sent_b = halves_of(along_z(term_b, "sum_b_z"), [kept_cot])
    both_a = add_far(kept_a, swap(sent_a, "yh", "sum_a_y"), [near_b])
    got_a = along_z(both_a.reshape(chips, -1, hidden // 2), "sum_a_z")
    both_cot = add_far(kept_cot, swap(sent_cot, "yh", "sum_cot_y"))
    pre_b, hidden_b = finish_b(near_b, swap(sent_b, "yh", "sum_b_y"), bias_half)
    copies_a = finish_a(got_a, bias_half, chips, [pre_b])
    full_a = gather_near(copies_a, "all_a")
    got_cot = along_z(both_cot.reshape(chips, -1, hidden // 2), "sum_cot_z")
    copies_back = finish_back(got_cot, pre_b, chips, [copies_a])

    parts_a = down(full_a, weight_out, plain, x_b, [copies_back])
    full_back = gather_near(copies_back, "all_back", [parts_a])
    full_b = gather_far(hidden_b, "all_b", [full_a[0][1], full_back[0][0]], [parts_a, full_back[0][1]])
    (grad_weight_out,) = grad(x_cot, full_b, 0, False, [parts_a])
    parts_back = down(full_back, weight_in, inner, x_b, [grad_weight_out])
    grad_weight_in, sums = grad(x_b, full_back, 1, True, [parts_back])
    output_a = sum_hidden(parts_a, bias_out, "row_out")
    grad_input = sum_hidden(parts_back, jnp.zeros_like(bias_out), "row_in")
    grad_bias_out = jnp.sum(x_cot.reshape(-1, x_cot.shape[-1]).astype(f32), axis=0)
    return (output_a, grad_input, grad_weight_in, sums[0], grad_weight_out, grad_bias_out)


def solution(mesh):
    fine = Mesh(mesh.devices.reshape(4, 2, 4, 2, 2), ("x", "yl", "z", "yh", "core"))
    return jax.shard_map(
        per_device,
        mesh=fine,
        in_specs=(
            P(ROW, COL),
            P(ROW, COL),
            P(ROW, COL),
            P(COL, ROW),
            P(ROW),
            P(ROW, COL),
            P(COL),
        ),
        out_specs=(
            P(ROW, COL),
            P(ROW, COL),
            P(COL, ROW),
            P(ROW),
            P(ROW, COL),
            P(COL),
        ),
        check_vma=False,
    )
```
